512 devices in a mesh: section: 4 (over x_hi, core), tensor: 8 (over z), dp: 16 (over y, x_lo).
Axes of the slice: x: 4 (x_hi: 2, x_lo: 2; x = x_hi * 2 + x_lo), y: 8, z: 8, core: 2. Of those that a mesh axis runs over, the one named last changes fastest.
Arguments:
- residual_in: bfloat16 [1, 256, 12288], P(None, ('section', 'tensor'), 'dp'), may hold values from -36 to 36
- up_first: bfloat16 [12288, 24576], P('dp', ('section', 'tensor')), may hold values from -0.0546875 to 0.0546875
- down_first: bfloat16 [24576, 12288], P(('section', 'tensor'), 'dp'), may hold values from -0.0390625 to 0.0390625
- gain_first: bfloat16 [12288], P('dp'), may hold values from 0.099609375 to 1.8984375
- up_second: bfloat16 [12288, 24576], P(('section', 'tensor'), 'dp'), may hold values from -0.0546875 to 0.0546875
- down_second: bfloat16 [24576, 12288], P('dp', ('section', 'tensor')), may hold values from -0.0390625 to 0.0390625
- gain_second: bfloat16 [12288], P(('section', 'tensor')), may hold values from 0.099609375 to 1.8984375
- cotangent: bfloat16 [1, 256, 12288], P(None, 'dp', ('section', 'tensor')), may hold values from -6 to 6
Outputs:
- residual_out: bfloat16 [1, 256, 12288], P(None, 'dp', ('section', 'tensor'))
- residual_grad: bfloat16 [1, 256, 12288], P(None, ('section', 'tensor'), 'dp')
The draws below stay inside these ranges and needn't reach their ends.
All inputs are finite; a program needn't handle non-finite values.
Results may differ from the reference program's by a relative error of at most 0.033.
Values may be sent and summed in bfloat16 or wider, within the bound.
No kernel may reach another device: no remote copies, remote signals or barrier semaphores. Data moves between devices by JAX's collectives and lax.ppermute only.
A program may use at most 64 MiB of HBM per device.

```python
import math
import jax
import jax.numpy as jnp
from jax import lax

D = 12288
FF = 24576
TOK = 256
MICRO = 1
N_SECTION = 4
N_TENSOR = 8
N_DP = 16


def draw_residual_in(key, part):
    key = jax.random.fold_in(key, 17)
    subkeys = jax.random.split(key, 3)
    shape = (MICRO, TOK, D)
    position = jnp.arange(D, dtype=jnp.float32) / (D - 1)
    values = jax.random.normal(subkeys[0], shape, jnp.float32)
    column = jnp.exp(jax.random.uniform(subkeys[1], (D,), jnp.float32, 0.0, math.log(3.0)))
    column = column * jnp.exp(math.log(3.0) * position)
    factor = 0.1
    values = jnp.clip(values, -4.0, 4.0)
    row_scale = jnp.exp(jax.random.uniform(subkeys[2], (MICRO, TOK, 1), jnp.float32, 0.0, math.log(10.0)))
    return (values * column * row_scale * factor).astype(jnp.bfloat16)


def block_levels(rng, dims, cuts, smallest, top_value):
    factor_of, own = 1.0, jax.random.fold_in(rng, 6)
    for axis_at, parts in cuts:
        heights = jnp.exp(jax.random.uniform(jax.random.fold_in(own, axis_at), (parts,), jnp.float32, smallest / len(cuts), top_value / len(cuts)))
        factor_of = factor_of * jnp.repeat(heights, dims[axis_at] // parts).reshape([-1 if axis == axis_at else 1 for axis in range(len(dims))])
    return factor_of


def normal_values(own_key, dims, scale, most, pieces=(), kind=jnp.bfloat16):
    level = block_levels(own_key, dims, pieces, -0.22, 0.18) if pieces else 1.0
    values = jax.random.normal(own_key, dims, jnp.float32) * scale * level
    return jnp.minimum(jnp.maximum(values, -most), most).astype(kind)


def setup_inputs(seed: int = 0) -> dict:
    streams_of = jax.random.split(jax.random.key(seed), 9)
    residual_in = draw_residual_in(jax.random.fold_in(streams_of[8], 71), 0)
    up_first = normal_values(streams_of[1], (D, FF), D ** -0.5, 0.0546875, ((0, 16), (1, 32)))
    down_first = normal_values(streams_of[2], (FF, D), FF ** -0.5, 0.0390625, ((0, 32), (1, 16)))
    gain_first = jnp.clip(1.0 + 0.18 * jax.random.normal(streams_of[3], (D,), jnp.float32), 0.099609375, 1.8984375).astype(jnp.bfloat16)
    up_second = normal_values(streams_of[4], (D, FF), D ** -0.5, 0.0546875, ((0, 32), (1, 16)))
    down_second = normal_values(streams_of[5], (FF, D), FF ** -0.5, 0.0390625, ((0, 16), (1, 32)))
    gain_second = jnp.clip(1.0 + 0.18 * jax.random.normal(streams_of[6], (D,), jnp.float32), 0.099609375, 1.8984375).astype(jnp.bfloat16)
    cotangent = normal_values(streams_of[7], (MICRO, TOK, D), 1.0, 6.0, ((1, 16), (2, 32)))
    return dict(residual_in=residual_in, up_first=up_first, down_first=down_first, gain_first=gain_first, up_second=up_second, down_second=down_second, gain_second=gain_second, cotangent=cotangent)


EPS = 1e-05
GELU_C0 = 0.7978845608028654
GELU_C1 = 0.044715

def gelu_value(hidden):
    inner = jnp.tanh(GELU_C0 * (hidden + GELU_C1 * hidden * hidden * hidden))
    return 0.5 * hidden * (1.0 + inner)

def gelu_slope(hidden):
    inner = jnp.tanh(GELU_C0 * (hidden + GELU_C1 * hidden * hidden * hidden))
    return 0.5 * (1.0 + inner) + 0.5 * hidden * (1.0 - inner * inner) * GELU_C0 * (1.0 + 3.0 * GELU_C1 * hidden * hidden)

def blocked(left, right, nblocks, along):
    width = left.shape[1] // nblocks
    out_cols = right.shape[1] if along == 0 else right.shape[0]

    def step(total, number):
        offset = (number * width).astype(jnp.int32)
        portion = lax.dynamic_slice_in_dim(left, offset, width, 1)
        if along == 0:
            weight = lax.dynamic_slice_in_dim(right, offset, width, 0)
            product = jnp.dot(portion, weight, preferred_element_type=jnp.float32)
        else:
            weight = lax.dynamic_slice_in_dim(right, offset, width, 1)
            product = lax.dot_general(portion, weight, (((1,), (1,)), ((), ())), preferred_element_type=jnp.float32)
        rounded = lax.optimization_barrier(product.astype(jnp.bfloat16))
        return (total + rounded.astype(jnp.float32), None)
    init = jnp.zeros((left.shape[0], out_cols), jnp.float32)
    total, _ = lax.scan(step, init, jnp.arange(nblocks, dtype=jnp.int32))
    return total

def norm_stats(values):
    floats = values.astype(jnp.float32)
    mean = lax.optimization_barrier(jnp.sum(floats, axis=1, keepdims=True)) / D
    square = lax.optimization_barrier(jnp.sum(floats * floats, axis=1, keepdims=True)) / D
    return (mean, lax.rsqrt(square - mean * mean + EPS))

def forward_block(values, w_up, w_down, gain, feat_blocks, unit_blocks):
    floats = values.astype(jnp.float32)
    mean, rstd = norm_stats(values)
    normed = ((floats - mean) * rstd * gain.astype(jnp.float32)).astype(jnp.bfloat16)
    hidden = blocked(normed, w_up, feat_blocks, 0)
    active = gelu_value(hidden).astype(jnp.bfloat16)
    mixed = blocked(active, w_down, unit_blocks, 0)
    return ((floats + mixed).astype(jnp.bfloat16), hidden, mean, rstd)

def backward_block(values, upstream, w_up, w_down, gain, hidden, mean, rstd, feat_blocks, unit_blocks):
    d_act = blocked(upstream, w_down, feat_blocks, 1)
    d_hid = (d_act * gelu_slope(hidden)).astype(jnp.bfloat16)
    d_norm = blocked(d_hid, w_up, unit_blocks, 1)
    nhat = (values.astype(jnp.float32) - mean) * rstd
    scaled = d_norm * gain.astype(jnp.float32)
    first_sum = lax.optimization_barrier(jnp.sum(scaled, axis=1, keepdims=True)) / D
    second_sum = lax.optimization_barrier(jnp.sum(scaled * nhat, axis=1, keepdims=True)) / D
    result = upstream.astype(jnp.float32) + rstd * (scaled - first_sum - nhat * second_sum)
    return result.astype(jnp.bfloat16)

def reference(residual_in, up_first, down_first, gain_first, up_second, down_second, gain_second, cotangent):
    joined_blocks = N_SECTION * N_TENSOR
    outputs = []
    gradients = []
    for micro_index in range(MICRO):
        values = residual_in[micro_index]
        middle, hidden_a, mean_a, rstd_a = forward_block(values, up_first, down_first, gain_first, N_DP, joined_blocks)
        final, hidden_b, mean_b, rstd_b = forward_block(middle, up_second, down_second, gain_second, joined_blocks, N_DP)
        middle_grad = backward_block(middle, cotangent[micro_index], up_second, down_second, gain_second, hidden_b, mean_b, rstd_b, joined_blocks, N_DP)
        input_grad = backward_block(values, middle_grad, up_first, down_first, gain_first, hidden_a, mean_a, rstd_a, N_DP, joined_blocks)
        outputs.append(final)
        gradients.append(input_grad)
    return (jnp.stack(outputs), jnp.stack(gradients))
```

```python
import jax
import jax.numpy as jnp
from jax import lax
from jax.sharding import Mesh, PartitionSpec as P

D = 12288
EPS = 1e-05
GELU_C0 = 0.7978845608028654
GELU_C1 = 0.044715
BF = jnp.bfloat16
F32 = jnp.float32
NAMES = ("xh", "core", "z", "y", "xl")
SIZES = (2, 2, 8, 8, 2)
ROW = ("xh", "z")
DP = ("y", "xl")
LANES = 128


def gelu_value(hidden):
    inner = jnp.tanh(GELU_C0 * (hidden + GELU_C1 * hidden * hidden * hidden))
    return 0.5 * hidden * (1.0 + inner)


def gelu_slope(hidden):
    inner = jnp.tanh(GELU_C0 * (hidden + GELU_C1 * hidden * hidden * hidden))
    return 0.5 * (1.0 + inner) + 0.5 * hidden * (1.0 - inner * inner) * GELU_C0 * (
        1.0 + 3.0 * GELU_C1 * hidden * hidden
    )


def dot(left, right):
    return jnp.dot(left, right, preferred_element_type=F32)


def contract_cols(left, right):
    return lax.dot_general(left, right, (((1,), (1,)), ((), ())), preferred_element_type=F32)


def split3(value):
    high = lax.reduce_precision(value, 8, 7)
    rest = value - high
    mid = lax.reduce_precision(rest, 8, 7)
    return high.astype(BF), mid.astype(BF), (rest - mid).astype(BF)


def pack_columns(columns):
    rows = columns[0].shape[0]
    parts = [piece[:, None] for column in columns for piece in split3(column)]
    parts.append(jnp.zeros((rows, LANES - len(parts)), BF))
    return jnp.concatenate(parts, axis=1)


def read_columns(block, count):
    floats = block.astype(F32)
    return [
        floats[:, 3 * k] + floats[:, 3 * k + 1] + floats[:, 3 * k + 2] for k in range(count)
    ]


def exchange(blocks, axis):
    return lax.all_to_all(blocks, axis, 0, 0)


def send_all(rows, axis, count):
    return exchange(jnp.broadcast_to(rows[None], (count,) + rows.shape), axis)


def gather_row(rows):
    part = send_all(rows, ROW, 16).reshape(16 * rows.shape[0], rows.shape[1])
    return lax.all_gather(part, "core", axis=0, tiled=True)


def pair_sum(values, width):
    half = exchange(values.reshape(2, 128, values.shape[1]), "core").astype(F32)
    total = half[0] + half[1]
    return total


def scatter_row(values, columns):
    width = values.shape[1]
    packed = jnp.concatenate([values, pack_columns(columns)], axis=1)
    total = pair_sum(packed, width)
    sums = read_columns(total[:, width:], len(columns))
    packed = jnp.concatenate([total[:, :width].astype(BF), pack_columns(sums)], axis=1)
    got = jnp.sum(exchange(packed.reshape(16, 8, width + LANES), ROW).astype(F32), axis=0)
    return got[:, :width], read_columns(got[:, width:], len(columns))


def swap_order(rows):
    blocks = rows.reshape(2, 2, 64, rows.shape[1])
    return jnp.transpose(blocks, (1, 0, 2, 3)).reshape(256, rows.shape[1])


def crossing(which):
    pairs = []
    for st in range(32):
        for group in range(16):
            target = (2 * group + (st + which) % 2) * 16 + st // 2
            pairs.append((st * 16 + group, target))
    return pairs


def cross(first, second):
    odd = lax.axis_index("z") % 2 == 1
    sent = (jnp.where(odd, second, first), jnp.where(odd, first, second))
    got = [lax.ppermute(sent[which], NAMES, crossing(which)) for which in range(2)]
    return jnp.where(odd, got[1], got[0]), jnp.where(odd, got[0], got[1])


def per_device(
    residual_in, up_first, down_first, gain_first, up_second, down_second, gain_second, cotangent
):
    gain_a = gain_first.astype(F32)
    gain_b = gain_second.astype(F32)
    own_rows = residual_in[0].astype(F32)
    cot_rows = cotangent[0]

    gain_up_a = dot(jnp.broadcast_to(gain_first[None], (8, 768)), up_first)[0]
    down_sum = jnp.sum(down_first.astype(F32), axis=1)
    gain_up_b = dot(jnp.broadcast_to(gain_second[None], (8, 384)), up_second)[0]

    stats = pack_columns([jnp.sum(own_rows, axis=1), jnp.sum(own_rows * own_rows, axis=1)])
    stats = jnp.concatenate([stats, jnp.zeros((16, LANES), BF)], axis=0)
    high_a, low_a, _ = split3(gain_up_a)
    high_d, low_d, _ = split3(down_sum)
    weights = jnp.concatenate([high_a, low_a, high_d, low_d]).reshape(8, 384)
    message = jnp.concatenate([jnp.concatenate([cot_rows, weights], axis=0), stats], axis=1)
    got = send_all(message, DP, 16)
    cot_all = got[:, :16, :384].reshape(256, 384)
    sums = jnp.sum(got[:, :8, 384:].astype(F32), axis=0)
    row_sum, square = read_columns(sums, 2)
    mean_a = (row_sum / D)[:, None]
    rstd_a = lax.rsqrt((square / D)[:, None] - mean_a * mean_a + EPS)
    totals = jnp.sum(got[:, 16:, :384].astype(F32), axis=0).reshape(4, 768)
    gain_up_a = totals[0] + totals[1]
    down_sum = totals[2] + totals[3]
    nhat_a = (own_rows - mean_a) * rstd_a
    normed = (nhat_a * gain_a).astype(BF)

    high_b, low_b, _ = split3(gain_up_b)
    extra = jnp.concatenate([high_b, low_b]).reshape(8, 384)
    gathered = gather_row(jnp.concatenate([normed, extra], axis=1))
    totals = jnp.sum(gathered[:, 768:].reshape(32, 8, 384).astype(F32), axis=0).reshape(2, 1536)
    gain_up_b = totals[0] + totals[1]
    part = dot(gathered[:, :768], up_first).astype(BF)
    hidden_a = jnp.sum(exchange(part.reshape(16, 16, 768), DP).astype(F32), axis=0)
    active = send_all(gelu_value(hidden_a).astype(BF), DP, 16).reshape(256, 768)
    part = dot(active, down_first).astype(BF)
    shift = jnp.sum(active.astype(F32) * down_sum, axis=1)
    mixed, (shift,) = scatter_row(part, [shift])
    middle_rows = (own_rows + mixed).astype(BF)
    mean_rows = mean_a[:, 0] + shift / D

    mean_cols = pack_columns([mean_rows])
    first, second = cross(
        jnp.concatenate([middle_rows[:, :384], mean_cols], axis=1),
        jnp.concatenate([middle_rows[:, 384:], mean_cols], axis=1),
    )
    middle_own = jnp.concatenate([first, second], axis=0)
    middle_all = swap_order(send_all(middle_own, DP, 16).reshape(256, 512))
    mean_all = read_columns(middle_all[:, 384:], 1)[0][:, None]
    mean_own = read_columns(middle_own[:, 384:], 1)[0][:, None]
    middle_own = middle_own[:, :384].astype(F32)
    centred = middle_all[:, :384].astype(F32) - mean_all
    spread = jnp.sum(centred * centred, axis=1)
    part = jnp.concatenate(
        [
            dot((centred * gain_b).astype(BF), up_second).astype(BF),
            contract_cols(swap_order(cot_all), down_second).astype(BF),
        ],
        axis=1,
    )
    both, (spread,) = scatter_row(part, [spread])
    rstd_rows = lax.rsqrt(spread / D + EPS)
    hidden_b = both[:, :1536] * rstd_rows[:, None]
    active_b = gelu_value(hidden_b).astype(BF)
    d_hid_b = (both[:, 1536:] * gelu_slope(hidden_b)).astype(BF)
    d_hid_float = d_hid_b.astype(F32)
    cols = pack_columns(
        [
            jnp.sum(d_hid_float * gain_up_b, axis=1),
            jnp.sum(d_hid_float * hidden_b, axis=1),
            rstd_rows,
        ]
    )
    gathered = gather_row(jnp.concatenate([active_b, d_hid_b, cols], axis=1))
    part = jnp.concatenate(
        [
            dot(gathered[:, :1536], down_second).astype(BF),
            contract_cols(gathered[:, 1536:3072], up_second).astype(BF),
            gathered[:, 3072:],
        ],
        axis=1,
    )
    got = exchange(swap_order(part).reshape(16, 16, 896), DP)
    sums = jnp.sum(got.astype(F32), axis=0)
    residual_out = (middle_own + sums[:, :384]).astype(BF)
    sum_one, sum_two = read_columns(sums[:, 768:], 2)
    rstd_own = read_columns(got[0, :, 768:], 3)[2][:, None]
    nhat_b = (middle_own - mean_own) * rstd_own
    grad_own = cot_rows.astype(F32) + rstd_own * (
        sums[:, 384:768] * gain_b - (sum_one / D)[:, None] - nhat_b * (sum_two / D)[:, None]
    )
    grad_own = grad_own.astype(BF)

    first, second = cross(grad_own[:8], grad_own[8:])
    grad_rows = jnp.concatenate([first, second], axis=1)
    part = contract_cols(gather_row(grad_rows), down_first).astype(BF)
    d_act_a = jnp.sum(exchange(part.reshape(16, 16, 768), DP).astype(F32), axis=0)
    d_hid_a = (d_act_a * gelu_slope(hidden_a)).astype(BF)
    d_hid_float = d_hid_a.astype(F32)
    cols = pack_columns(
        [jnp.sum(d_hid_float * gain_up_a, axis=1), jnp.sum(d_hid_float * hidden_a, axis=1)]
    )
    gathered = send_all(jnp.concatenate([d_hid_a, cols], axis=1), DP, 16).reshape(256, 896)
    part = contract_cols(gathered[:, :768], up_first).astype(BF)
    sums = read_columns(gathered[:, 768:], 2)
    d_norm_a, (sum_one, sum_two) = scatter_row(part, sums)
    result = grad_rows.astype(F32) + rstd_a * (
        d_norm_a * gain_a - (sum_one / D)[:, None] - nhat_a * (sum_two / D)[:, None]
    )
    return residual_out[None], result.astype(BF)[None]


def solution(mesh):
    fine = Mesh(mesh.devices.reshape(SIZES), NAMES)
    row = ("xh", "core", "z")
    return jax.shard_map(
        per_device,
        mesh=fine,
        in_specs=(
            P(None, row, DP),
            P(DP, row),
            P(row, DP),
            P(DP),
            P(row, DP),
            P(DP, row),
            P(row),
            P(None, DP, row),
        ),
        out_specs=(P(None, DP, row), P(None, row, DP)),
        check_vma=False,
    )
```

```python
import jax
import jax.numpy as jnp
from jax import lax
from jax.sharding import Mesh, PartitionSpec as P

D = 12288
EPS = 1e-05
GELU_C0 = 0.7978845608028654
GELU_C1 = 0.044715
BF = jnp.bfloat16
F32 = jnp.float32
NAMES = ("xh", "core", "z", "y", "xl")
SIZES = (2, 2, 8, 8, 2)
ROW = ("xh", "z")
DP = ("y", "xl")
LANES = 128


def gelu_value(hidden):
    inner = jnp.tanh(GELU_C0 * (hidden + GELU_C1 * hidden * hidden * hidden))
    return 0.5 * hidden * (1.0 + inner)


def gelu_slope(hidden):
    inner = jnp.tanh(GELU_C0 * (hidden + GELU_C1 * hidden * hidden * hidden))
    return 0.5 * (1.0 + inner) + 0.5 * hidden * (1.0 - inner * inner) * GELU_C0 * (
        1.0 + 3.0 * GELU_C1 * hidden * hidden
    )


def dot(left, right):
    return jnp.dot(left, right, preferred_element_type=F32)


def contract_cols(left, right):
    return lax.dot_general(left, right, (((1,), (1,)), ((), ())), preferred_element_type=F32)


def row_dot(values, row):
    return lax.dot_general(
        values,
        jnp.broadcast_to(row, (LANES, values.shape[1])),
        (((1,), (1,)), ((), ())),
        precision=lax.Precision.HIGHEST,
        preferred_element_type=F32,
    )


def split3(value):
    high = lax.reduce_precision(value, 8, 7)
    rest = value - high
    mid = lax.reduce_precision(rest, 8, 7)
    return high, mid, rest - mid


def pack(columns):
    rows = columns[0].shape[0]
    lane = lax.broadcasted_iota(jnp.int32, (rows, LANES), 1)
    block = jnp.zeros((rows, LANES), F32)
    for number, column in enumerate(columns):
        for part, piece in enumerate(split3(column)):
            block = jnp.where(lane == 3 * number + part, piece, block)
    return block.astype(BF)


def unpack(floats, number):
    at = 3 * number
    return floats[..., at : at + 1] + floats[..., at + 1 : at + 2] + floats[..., at + 2 : at + 3]


def exchange(blocks, axis):
    return lax.all_to_all(blocks, axis, 0, 0)


def send_all(rows, axis):
    got = exchange(jnp.broadcast_to(rows[None], (16,) + rows.shape), axis)
    return got.reshape(16 * rows.shape[0], rows.shape[1])


def both_cores(values):
    return lax.all_gather(values, "core", axis=0, tiled=False)


def tile_rows(vector, rows):
    block = vector.reshape(-1, LANES)
    return jnp.concatenate([block, jnp.zeros((rows - block.shape[0], LANES), vector.dtype)], axis=0)


def crossing():
    pairs = []
    for xh in range(2):
        for core in range(2):
            for z in range(8):
                for group in range(16):
                    source = ((xh * 2 + core) * 8 + z) * 16 + group
                    pairs.append((source, (2 * group + core) * 16 + xh * 8 + z))
    return pairs


def per_device(
    residual_in, up_first, down_first, gain_first, up_second, down_second, gain_second, cotangent
):
    core = lax.axis_index("core")
    chunk = lax.axis_index("xh") * 8 + lax.axis_index("z")
    own_row = (lax.axis_index("xh") * 16 + core * 8 + lax.axis_index("z")) * 8
    gain_a = gain_first.astype(F32)
    gain_b = gain_second.astype(F32)
    x_own = residual_in[0]
    cot_own = cotangent[0]

    u_a = dot(jnp.broadcast_to(gain_first[None], (8, 768)), up_first)[0].astype(BF)
    u_b = dot(jnp.broadcast_to(gain_second[None], (8, 384)), up_second)[0].astype(BF)
    d_high, d_mid, _ = split3(contract_cols(jnp.ones((8, 768), BF), down_first)[0])

    floats = x_own.astype(F32)
    centre = jnp.sum(floats, axis=1, keepdims=True) / 768
    spread = jnp.sum((floats - centre) * (floats - centre), axis=1, keepdims=True)
    u_b = tile_rows(u_b, 16)
    message = jnp.concatenate([x_own, pack([centre, spread]), u_b[:8], u_b[8:]], axis=1)
    got = both_cores(send_all(message, ROW))
    gain_up_b = jnp.sum(got[:, :, 896:].reshape(32, 8, 256).astype(F32), axis=0)
    gain_up_b = jnp.concatenate([gain_up_b[:, :128], gain_up_b[:4, 128:]], axis=0).reshape(2, 768)
    gain_up_b = jnp.where(core == 0, gain_up_b[:1], gain_up_b[1:])
    x_all = jnp.transpose(got.reshape(2, 2, 64, 1152), (1, 0, 2, 3)).reshape(256, 1152)
    x_cols = x_all[:, 768:896]
    x_all = x_all[:, :768]

    centred = (x_all.astype(F32) - unpack(x_cols.astype(F32), 0)) * gain_a
    part = dot(centred.astype(BF), up_first).astype(BF)
    message = jnp.concatenate(
        [
            part.reshape(16, 16, 768),
            x_cols.reshape(16, 16, LANES),
            jnp.broadcast_to(tile_rows(u_a, 16)[None], (16, 16, LANES)),
        ],
        axis=2,
    )
    got = exchange(message, DP)
    cols = got[:, :, 768:896].astype(F32)
    centres = unpack(cols, 0)
    mean_a = jnp.mean(centres, axis=0)
    off = centres - mean_a
    var_a = (jnp.sum(unpack(cols, 1), axis=0) + 768 * jnp.sum(off * off, axis=0)) / D
    rstd_a = lax.rsqrt(var_a + EPS)
    u_all = got[:, :6, 896:].reshape(16, 1, 768).astype(F32)
    gain_up_a = jnp.sum(u_all, axis=0)
    hidden_a = rstd_a * jnp.sum(got[:, :, :768].astype(F32) + off * u_all, axis=0)
    message = jnp.concatenate(
        [
            gelu_value(hidden_a).astype(BF),
            pack([mean_a, rstd_a]),
            jnp.concatenate([tile_rows(d_high, 8), tile_rows(d_mid, 8)], axis=0).astype(BF),
        ],
        axis=1,
    )
    got = send_all(message, DP)
    stats_a = got[:, 768:896]
    sums = jnp.sum(got[:, 896:].reshape(16, 2, 8, LANES).astype(F32), axis=(0, 1))
    down_sum = sums[:6].reshape(1, 768)
    active = got[:, :768]
    part = dot(active, down_first).astype(BF)
    shift = row_dot(active.astype(F32), down_sum) + unpack(stats_a.astype(F32), 0) * (D / 32)
    cols = pack([shift])
    message = jnp.stack(
        [
            jnp.concatenate([part[:, :384], cols], axis=1),
            jnp.concatenate([part[:, 384:], cols], axis=1),
        ]
    )
    got = exchange(message, "core")
    part = jnp.sum(got[:, :, :384].astype(F32), axis=0).astype(BF)
    message = jnp.concatenate([part, got[0, :, 384:], got[1, :, 384:]], axis=1)
    sums = jnp.sum(exchange(message.reshape(16, 16, 640), ROW).astype(F32), axis=0)
    mean_b = (unpack(sums[:, 384:512], 0) + unpack(sums[:, 512:], 0)) / D
    rows = lax.dynamic_slice_in_dim(x_all, chunk * 16, 16, 0)
    rows = jnp.where(core == 0, rows[:, :384], rows[:, 384:]).astype(F32)
    middle = (rows + sums[:, :384]).astype(BF)

    crossed = lax.ppermute(jnp.concatenate([middle, pack([mean_b])], axis=1), NAMES, crossing())
    middle_own = crossed[:, :384].astype(F32)
    mean_own = unpack(crossed[:, 384:].astype(F32), 0)
    got = send_all(jnp.concatenate([crossed, cot_own], axis=1), DP)
    cot_all = got[:, 512:]
    centred = got[:, :384].astype(F32) - unpack(got[:, 384:512].astype(F32), 0)
    cols = pack([row_dot(centred * centred, jnp.ones((1, 384), F32))])
    centred = (centred * gain_b).astype(BF)
    message = jnp.stack(
        [
            jnp.concatenate(
                [
                    dot(centred, up_second[:, at : at + 768]).astype(BF),
                    contract_cols(cot_all, down_second[at : at + 768]).astype(BF),
                    cols,
                ],
                axis=1,
            )
            for at in (0, 768)
        ]
    )
    got = exchange(message, "core")
    part = jnp.sum(got[:, :, :1536].astype(F32), axis=0).astype(BF)
    message = jnp.concatenate([part, got[0, :, 1536:], got[1, :, 1536:]], axis=1)
    sums = jnp.sum(exchange(message.reshape(16, 16, 1792), ROW).astype(F32), axis=0)
    spread = unpack(sums[:, 1536:1664], 0) + unpack(sums[:, 1664:], 0)
    rstd_b = lax.rsqrt(spread / D + EPS)
    hidden_b = sums[:, :768] * rstd_b
    active_b = gelu_value(hidden_b).astype(BF)
    d_hid_b = (sums[:, 768:1536] * gelu_slope(hidden_b)).astype(BF)
    floats = d_hid_b.astype(F32)
    cols = pack(
        [
            jnp.sum(floats * gain_up_b, axis=1, keepdims=True),
            jnp.sum(floats * hidden_b, axis=1, keepdims=True),
            rstd_b,
        ]
    )
    got = both_cores(send_all(jnp.concatenate([d_hid_b, cols], axis=1), ROW))
    part = contract_cols(got[0, :, :768], up_second[:, :768])
    part = part + contract_cols(got[1, :, :768], up_second[:, 768:])
    message = jnp.concatenate([part.astype(BF), got[0, :, 768:], got[1, :, 768:]], axis=1)
    got = exchange(message.reshape(16, 16, 640), DP)
    sums = jnp.sum(got.astype(F32), axis=0)
    sum_one = unpack(sums[:, 384:512], 0) + unpack(sums[:, 512:], 0)
    sum_two = unpack(sums[:, 384:512], 1) + unpack(sums[:, 512:], 1)
    rstd_own = unpack(got[0, :, 384:512].astype(F32), 2)
    nhat_b = (middle_own - mean_own) * rstd_own
    grad_own = cot_own.astype(F32) + rstd_own * (
        sums[:, :384] * gain_b - sum_one / D - nhat_b * (sum_two / D)
    )

    crossed = lax.ppermute(
        grad_own.astype(BF), NAMES, [(target, source) for source, target in crossing()]
    )
    got = send_all(jnp.concatenate([crossed, active_b], axis=1), ROW)
    grad_all = both_cores(got[:, :384])
    active_all = both_cores(got[:, 384:])
    part = contract_cols(grad_all[0], down_first[:, :384])
    part = part + contract_cols(grad_all[1], down_first[:, 384:])
    part_b = dot(active_all[0], down_second[:768]) + dot(active_all[1], down_second[768:])
    message = jnp.concatenate([part.astype(BF), part_b.astype(BF)], axis=1)
    sums = jnp.sum(exchange(message.reshape(16, 16, 1152), DP).astype(F32), axis=0)
    residual_out = (middle_own + sums[:, 768:]).astype(BF)
    d_hid_a = (sums[:, :768] * gelu_slope(hidden_a)).astype(BF)
    floats = d_hid_a.astype(F32)
    cols = pack(
        [
            jnp.sum(floats * gain_up_a, axis=1, keepdims=True),
            jnp.sum(floats * hidden_a, axis=1, keepdims=True),
        ]
    )
    got = send_all(jnp.concatenate([d_hid_a, cols], axis=1), DP)
    part = contract_cols(got[:, :768], up_first).astype(BF)
    message = jnp.concatenate([part, got[:, 768:]], axis=1).reshape(2, 2, 64, 896)
    got = exchange(jnp.transpose(message, (1, 0, 2, 3)).reshape(2, 128, 896), "core")
    part = jnp.sum(got[:, :, :768].astype(F32), axis=0).astype(BF)
    message = jnp.concatenate([part, got[0, :, 768:], got[1, :, 768:]], axis=1)
    sums = jnp.sum(exchange(message.reshape(16, 8, 1024), ROW).astype(F32), axis=0)
    sum_one = unpack(sums[:, 768:896], 0) + unpack(sums[:, 896:], 0)
    sum_two = unpack(sums[:, 768:896], 1) + unpack(sums[:, 896:], 1)
    stats = lax.dynamic_slice_in_dim(stats_a, own_row, 8, 0).astype(F32)
    rstd = unpack(stats, 1)
    nhat_a = (x_own.astype(F32) - unpack(stats, 0)) * rstd
    upstream = lax.dynamic_slice_in_dim(grad_all, own_row, 8, 1).astype(F32)
    upstream = jnp.concatenate([upstream[0], upstream[1]], axis=1)
    result = upstream + rstd * (sums[:, :768] * gain_a - sum_one / D - nhat_a * (sum_two / D))
    return residual_out[None], result.astype(BF)[None]


def solution(mesh):
    fine = Mesh(mesh.devices.reshape(SIZES), NAMES)
    row = ("xh", "core", "z")
    return jax.shard_map(
        per_device,
        mesh=fine,
        in_specs=(
            P(None, row, DP),
            P(DP, row),
            P(row, DP),
            P(DP),
            P(row, DP),
            P(DP, row),
            P(row),
            P(None, DP, row),
        ),
        out_specs=(P(None, DP, row), P(None, row, DP)),
        check_vma=False,
    )
```

```python
import jax
import jax.numpy as jnp
from jax import lax
from jax.sharding import Mesh, PartitionSpec as P

D = 12288
EPS = 1e-05
GELU_C0 = 0.7978845608028654
GELU_C1 = 0.044715
BF = jnp.bfloat16
F32 = jnp.float32
NAMES = ("xh", "core", "z", "y", "xl")
SIZES = (2, 2, 8, 8, 2)
ROW = ("xh", "z")
DP = ("y", "xl")
LANES = 128


def gelu_value(hidden):
    inner = jnp.tanh(GELU_C0 * (hidden + GELU_C1 * hidden * hidden * hidden))
    return 0.5 * hidden * (1.0 + inner)


def gelu_slope(hidden):
    inner = jnp.tanh(GELU_C0 * (hidden + GELU_C1 * hidden * hidden * hidden))
    return 0.5 * (1.0 + inner) + 0.5 * hidden * (1.0 - inner * inner) * GELU_C0 * (
        1.0 + 3.0 * GELU_C1 * hidden * hidden
    )


def dot(left, right):
    return jnp.dot(left, right, preferred_element_type=F32)


def contract_cols(left, right):
    return lax.dot_general(left, right, (((1,), (1,)), ((), ())), preferred_element_type=F32)


def row_dot(values, row):
    return lax.dot_general(
        values,
        jnp.broadcast_to(row, (LANES, values.shape[1])),
        (((1,), (1,)), ((), ())),
        precision=lax.Precision.HIGHEST,
        preferred_element_type=F32,
    )


def split3(value):
    high = lax.reduce_precision(value, 8, 7)
    rest = value - high
    mid = lax.reduce_precision(rest, 8, 7)
    return high, mid, rest - mid


def pack(columns, first=0):
    rows = columns[0].shape[0]
    lane = lax.broadcasted_iota(jnp.int32, (rows, LANES), 1) - first
    block = jnp.zeros((rows, LANES), F32)
    for number, column in enumerate(columns):
        for part, piece in enumerate(split3(column)):
            block = jnp.where(lane == 3 * number + part, piece, block)
    return block.astype(BF)


def unpack(floats, number):
    at = 3 * number
    return floats[..., at : at + 1] + floats[..., at + 1 : at + 2] + floats[..., at + 2 : at + 3]


def unpack_pair(floats, number):
    return unpack(floats, number) + unpack(floats[..., 64:], number)


def exchange(blocks, axis):
    return lax.all_to_all(blocks, axis, 0, 0)


def send_all(rows, axis):
    got = exchange(jnp.broadcast_to(rows[None], (16,) + rows.shape), axis)
    return got.reshape(16 * rows.shape[0], rows.shape[1])


def both_cores(values):
    return lax.all_gather(values, "core", axis=0, tiled=False)


def tile_rows(vector, rows):
    block = vector.reshape(-1, LANES)
    return jnp.concatenate([block, jnp.zeros((rows - block.shape[0], LANES), vector.dtype)], axis=0)


def crossing():
    pairs = []
    for xh in range(2):
        for core in range(2):
            for z in range(8):
                for group in range(16):
                    source = ((xh * 2 + core) * 8 + z) * 16 + group
                    pairs.append((source, (2 * group + core) * 16 + xh * 8 + z))
    return pairs


def per_device(
    residual_in, up_first, down_first, gain_first, up_second, down_second, gain_second, cotangent
):
    core = lax.axis_index("core")
    chunk = lax.axis_index("xh") * 8 + lax.axis_index("z")
    own_row = (lax.axis_index("xh") * 16 + core * 8 + lax.axis_index("z")) * 8
    gain_a = gain_first.astype(F32)
    gain_b = gain_second.astype(F32)
    x_own = residual_in[0]
    cot_own = cotangent[0]

    u_a = dot(jnp.broadcast_to(gain_first[None], (8, 768)), up_first)[0].astype(BF)
    u_b = dot(jnp.broadcast_to(gain_second[None], (8, 384)), up_second)[0].astype(BF)
    down_sum = contract_cols(jnp.ones((8, 768), BF), down_first)[0].astype(BF)
    sums_a = jnp.concatenate([tile_rows(u_a, 8), tile_rows(down_sum, 8)], axis=0)

    floats = x_own.astype(F32)
    centre = jnp.sum(floats, axis=1, keepdims=True) / 768
    spread = jnp.sum((floats - centre) * (floats - centre), axis=1, keepdims=True)
    message = jnp.concatenate([x_own, pack([centre, spread])], axis=1)
    got = both_cores(send_all(message, ROW))
    x_all = jnp.transpose(got.reshape(2, 2, 64, 896), (1, 0, 2, 3)).reshape(256, 896)
    x_cols = x_all[:, 768:]
    x_all = x_all[:, :768]

    centred = (x_all.astype(F32) - unpack(x_cols.astype(F32), 0)) * gain_a
    part = dot(centred.astype(BF), up_first).astype(BF)
    message = jnp.concatenate(
        [
            part.reshape(16, 16, 768),
            x_cols.reshape(16, 16, LANES),
            jnp.broadcast_to(sums_a[None], (16, 16, LANES)),
        ],
        axis=2,
    )
    got = exchange(message, DP)
    cols = got[:, :, 768:896].astype(F32)
    centres = unpack(cols, 0)
    mean_a = jnp.mean(centres, axis=0)
    off = centres - mean_a
    var_a = (jnp.sum(unpack(cols, 1), axis=0) + 768 * jnp.sum(off * off, axis=0)) / D
    rstd_a = lax.rsqrt(var_a + EPS)
    u_all = got[:, :6, 896:].reshape(16, 1, 768).astype(F32)
    gain_up_a = jnp.sum(u_all, axis=0)
    down_sum = jnp.sum(got[:, 8:14, 896:].astype(F32), axis=0).reshape(1, 768)
    hidden_a = rstd_a * jnp.sum(got[:, :, :768].astype(F32) + off * u_all, axis=0)
    active = gelu_value(hidden_a).astype(BF)
    got = send_all(jnp.concatenate([active, pack([mean_a, rstd_a])], axis=1), DP)
    stats_a = got[:, 768:]
    active = got[:, :768]
    part = dot(active, down_first).astype(BF)
    shift = row_dot(active.astype(F32), down_sum) + unpack(stats_a.astype(F32), 0) * (D / 32)
    cols = pack([shift], 64 * core)
    message = jnp.stack(
        [
            jnp.concatenate([part[:, :384], cols], axis=1),
            jnp.concatenate([part[:, 384:], cols], axis=1),
        ]
    )
    got = exchange(message, "core")
    part = jnp.sum(got.astype(F32), axis=0).astype(BF)
    sums = jnp.sum(exchange(part.reshape(16, 16, 512), ROW).astype(F32), axis=0)
    centre = unpack_pair(sums[:, 384:], 0) / D
    rows = lax.dynamic_slice_in_dim(x_all, chunk * 16, 16, 0)
    rows = jnp.where(core == 0, rows[:, :384], rows[:, 384:]).astype(F32)
    middle = (rows + sums[:, :384]).astype(BF)

    crossed = lax.ppermute(jnp.concatenate([middle, pack([centre])], axis=1), NAMES, crossing())
    middle_own = crossed[:, :384].astype(F32)
    got = send_all(jnp.concatenate([crossed, cot_own], axis=1), DP)
    cot_all = got[:, 512:]
    centred = got[:, :384].astype(F32) - unpack(got[:, 384:512].astype(F32), 0)
    ones = jnp.ones((1, 384), F32)
    cols = pack([row_dot(centred * centred, ones), row_dot(centred, ones)], 64 * core)
    centred = (centred * gain_b).astype(BF)
    message = jnp.stack(
        [
            jnp.concatenate(
                [
                    dot(centred, up_second[:, at : at + 768]).astype(BF),
                    contract_cols(cot_all, down_second[at : at + 768]).astype(BF),
                    cols,
                    jnp.tile(tile_rows(u_b[at : at + 768], 16), (16, 1)),
                ],
                axis=1,
            )
            for at in (0, 768)
        ]
    )
    got = exchange(message, "core")
    part = jnp.sum(got.astype(F32), axis=0).astype(BF)
    sums = jnp.sum(exchange(part.reshape(16, 16, 1792), ROW).astype(F32), axis=0)
    gain_up_b = sums[:6, 1664:].reshape(1, 768)
    off = unpack_pair(sums[:, 1536:1664], 1) / D
    rstd_b = lax.rsqrt(unpack_pair(sums[:, 1536:1664], 0) / D - off * off + EPS)
    hidden_b = (sums[:, :768] - off * gain_up_b) * rstd_b
    active_b = gelu_value(hidden_b).astype(BF)
    d_hid_b = (sums[:, 768:1536] * gelu_slope(hidden_b)).astype(BF)
    floats = d_hid_b.astype(F32)
    cols = pack(
        [
            jnp.sum(floats * gain_up_b, axis=1, keepdims=True),
            jnp.sum(floats * hidden_b, axis=1, keepdims=True),
            rstd_b,
            off,
        ],
        64 * core,
    )
    got = send_all(jnp.concatenate([d_hid_b, cols, active_b], axis=1), ROW)
    active = both_cores(got[:, 896:])
    got = both_cores(got[:, :896])
    part = contract_cols(got[0, :, :768], up_second[:, :768])
    part = part + contract_cols(got[1, :, :768], up_second[:, 768:])
    cols = got[0, :, 768:] + got[1, :, 768:]
    part_b = dot(active[0], down_second[:768]) + dot(active[1], down_second[768:])
    message = jnp.concatenate([part.astype(BF), cols, part_b.astype(BF)], axis=1)
    got = exchange(message.reshape(16, 16, 896), DP)
    sums = jnp.sum(got.astype(F32), axis=0)
    residual_out = (middle_own + sums[:, 512:]).astype(BF)
    sum_one = unpack_pair(sums[:, 384:512], 0)
    sum_two = unpack_pair(sums[:, 384:512], 1)
    cols = got[0, :, 384:512].astype(F32)
    rstd_own = unpack(cols, 2)
    mean_own = unpack(crossed[:, 384:].astype(F32), 0) + unpack(cols, 3)
    nhat_b = (middle_own - mean_own) * rstd_own
    grad_own = cot_own.astype(F32) + rstd_own * (
        sums[:, :384] * gain_b - sum_one / D - nhat_b * (sum_two / D)
    )

    crossed = lax.ppermute(
        grad_own.astype(BF), NAMES, [(target, source) for source, target in crossing()]
    )
    grad_all = both_cores(send_all(crossed, ROW))
    part = contract_cols(grad_all[0], down_first[:, :384])
    part = part + contract_cols(grad_all[1], down_first[:, 384:])
    sums = jnp.sum(exchange(part.astype(BF).reshape(16, 16, 768), DP).astype(F32), axis=0)
    d_hid_a = (sums * gelu_slope(hidden_a)).astype(BF)
    floats = d_hid_a.astype(F32)
    cols = pack(
        [
            jnp.sum(floats * gain_up_a, axis=1, keepdims=True),
            jnp.sum(floats * hidden_a, axis=1, keepdims=True),
        ],
        64 * core,
    )
    got = send_all(jnp.concatenate([d_hid_a, cols], axis=1), DP)
    part = contract_cols(got[:, :768], up_first).astype(BF)
    message = jnp.concatenate([part, got[:, 768:]], axis=1).reshape(2, 2, 64, 896)
    got = exchange(jnp.transpose(message, (1, 0, 2, 3)).reshape(2, 128, 896), "core")
    part = jnp.sum(got.astype(F32), axis=0).astype(BF)
    sums = jnp.sum(exchange(part.reshape(16, 8, 896), ROW).astype(F32), axis=0)
    sum_one = unpack_pair(sums[:, 768:], 0)
    sum_two = unpack_pair(sums[:, 768:], 1)
    stats = lax.dynamic_slice_in_dim(stats_a, own_row, 8, 0).astype(F32)
    rstd = unpack(stats, 1)
    nhat_a = (x_own.astype(F32) - unpack(stats, 0)) * rstd
    upstream = lax.dynamic_slice_in_dim(grad_all, own_row, 8, 1).astype(F32)
    upstream = jnp.concatenate([upstream[0], upstream[1]], axis=1)
    result = upstream + rstd * (sums[:, :768] * gain_a - sum_one / D - nhat_a * (sum_two / D))
    return residual_out[None], result.astype(BF)[None]


def solution(mesh):
    fine = Mesh(mesh.devices.reshape(SIZES), NAMES)
    row = ("xh", "core", "z")
    return jax.shard_map(
        per_device,
        mesh=fine,
        in_specs=(
            P(None, row, DP),
            P(DP, row),
            P(row, DP),
            P(DP),
            P(row, DP),
            P(DP, row),
            P(row),
            P(None, DP, row),
        ),
        out_specs=(P(None, DP, row), P(None, row, DP)),
        check_vma=False,
    )
```

```python
import jax
import jax.numpy as jnp
from jax import lax
from jax.sharding import Mesh, PartitionSpec as P

D = 12288
EPS = 1e-05
GELU_C0 = 0.7978845608028654
GELU_C1 = 0.044715
BF = jnp.bfloat16
F32 = jnp.float32
NAMES = ("xh", "core", "z", "y", "xl")
SIZES = (2, 2, 8, 8, 2)
ROW = ("xh", "z")
DP = ("y", "xl")
LANES = 128


def gelu_value(hidden):
    inner = jnp.tanh(GELU_C0 * (hidden + GELU_C1 * hidden * hidden * hidden))
    return 0.5 * hidden * (1.0 + inner)


def gelu_slope(hidden):
    inner = jnp.tanh(GELU_C0 * (hidden + GELU_C1 * hidden * hidden * hidden))
    return 0.5 * (1.0 + inner) + 0.5 * hidden * (1.0 - inner * inner) * GELU_C0 * (
        1.0 + 3.0 * GELU_C1 * hidden * hidden
    )


def dot(left, right):
    return jnp.dot(left, right, preferred_element_type=F32)


def contract_cols(left, right):
    return lax.dot_general(left, right, (((1,), (1,)), ((), ())), preferred_element_type=F32)


def row_dot(values, row):
    return lax.dot_general(
        values,
        jnp.broadcast_to(row, (LANES, values.shape[1])),
        (((1,), (1,)), ((), ())),
        precision=lax.Precision.HIGHEST,
        preferred_element_type=F32,
    )


def split3(value):
    high = lax.reduce_precision(value, 8, 7)
    rest = value - high
    mid = lax.reduce_precision(rest, 8, 7)
    return high, mid, rest - mid


def pack(columns, first=0):
    rows = columns[0].shape[0]
    lane = lax.broadcasted_iota(jnp.int32, (rows, LANES), 1) - first
    block = jnp.zeros((rows, LANES), F32)
    for number, column in enumerate(columns):
        for part, piece in enumerate(split3(column)):
            block = jnp.where(lane == 3 * number + part, piece, block)
    return block.astype(BF)


def unpack(floats, number):
    at = 3 * number
    return floats[..., at : at + 1] + floats[..., at + 1 : at + 2] + floats[..., at + 2 : at + 3]


def unpack_pair(floats, number):
    return unpack(floats, number) + unpack(floats[..., 64:], number)


def exchange(blocks, axis):
    return lax.all_to_all(blocks, axis, 0, 0)


def send_all(rows, axis):
    got = exchange(jnp.broadcast_to(rows[None], (16,) + rows.shape), axis)
    return got.reshape(16 * rows.shape[0], rows.shape[1])


def both_cores(values):
    return lax.all_gather(values, "core", axis=0, tiled=False)


def pair_sum(core, first, second):
    both = both_cores(jnp.where(core == 0, second, first))
    kept = jnp.where(core == 0, first, second)
    return (kept.astype(F32) + jnp.where(core == 0, both[1], both[0]).astype(F32)).astype(BF)


def tile_rows(vector, rows):
    block = vector.reshape(-1, LANES)
    return jnp.concatenate([block, jnp.zeros((rows - block.shape[0], LANES), vector.dtype)], axis=0)


def crossing():
    pairs = []
    for xh in range(2):
        for core in range(2):
            for z in range(8):
                for group in range(16):
                    source = ((xh * 2 + core) * 8 + z) * 16 + group
                    pairs.append((source, (2 * group + core) * 16 + xh * 8 + z))
    return pairs


def per_device(
    residual_in, up_first, down_first, gain_first, up_second, down_second, gain_second, cotangent
):
    core = lax.axis_index("core")
    chunk = lax.axis_index("xh") * 8 + lax.axis_index("z")
    own_row = (lax.axis_index("xh") * 16 + core * 8 + lax.axis_index("z")) * 8
    gain_a = gain_first.astype(F32)
    gain_b = gain_second.astype(F32)
    x_own = residual_in[0]
    cot_own = cotangent[0]

    u_a = dot(jnp.broadcast_to(gain_first[None], (8, 768)), up_first)[0].astype(BF)
    u_b = dot(jnp.broadcast_to(gain_second[None], (8, 384)), up_second)[0].astype(BF)
    down_sum = contract_cols(jnp.ones((8, 768), BF), down_first)[0].astype(BF)
    sums_a = jnp.concatenate([u_a.reshape(8, 96), down_sum.reshape(8, 96)], axis=0)
    sums_a = jnp.pad(sums_a, ((0, 0), (0, 32)))

    got = both_cores(send_all(x_own, ROW))
    x_all = jnp.transpose(got.reshape(2, 2, 64, 768), (1, 0, 2, 3)).reshape(256, 768)

    floats = x_all.astype(F32)
    centre = jnp.sum(floats, axis=1, keepdims=True) / 768
    centred = floats - centre
    x_cols = pack([centre, jnp.sum(centred * centred, axis=1, keepdims=True)], 96)
    lane = lax.broadcasted_iota(jnp.int32, (16, 16, LANES), 2)
    x_cols = jnp.where(lane < 96, sums_a, x_cols.reshape(16, 16, LANES))
    part = dot((centred * gain_a).astype(BF), up_first).astype(BF)
    got = exchange(jnp.concatenate([part.reshape(16, 16, 768), x_cols], axis=2), DP)
    cols = got[:, :, 864:].astype(F32)
    centres = unpack(cols, 0)
    mean_a = jnp.mean(centres, axis=0)
    off = centres - mean_a
    var_a = (jnp.sum(unpack(cols, 1), axis=0) + 768 * jnp.sum(off * off, axis=0)) / D
    rstd_a = lax.rsqrt(var_a + EPS)
    u_all = got[:, :8, 768:864].reshape(16, 1, 768).astype(F32)
    gain_up_a = jnp.sum(u_all, axis=0)
    down_sum = jnp.sum(got[:, 8:, 768:864].astype(F32), axis=0).reshape(1, 768)
    hidden_a = rstd_a * jnp.sum(got[:, :, :768].astype(F32) + off * u_all, axis=0)
    active = gelu_value(hidden_a).astype(BF)
    got = send_all(jnp.concatenate([active, pack([mean_a, rstd_a])], axis=1), DP)
    stats_a = got[:, 768:]
    active = got[:, :768]
    part = dot(active, down_first).astype(BF)
    shift = row_dot(active.astype(F32), down_sum) + unpack(stats_a.astype(F32), 0) * (D / 32)
    cols = pack([shift], 64 * core)
    part = pair_sum(
        core,
        jnp.concatenate([part[:, :384], cols], axis=1),
        jnp.concatenate([part[:, 384:], cols], axis=1),
    )
    sums = jnp.sum(exchange(part.reshape(16, 16, 512), ROW).astype(F32), axis=0)
    centre = unpack_pair(sums[:, 384:], 0) / D
    rows = lax.dynamic_slice_in_dim(x_all, chunk * 16, 16, 0)
    rows = jnp.where(core == 0, rows[:, :384], rows[:, 384:]).astype(F32)
    middle = (rows + sums[:, :384]).astype(BF)

    crossed = lax.ppermute(jnp.concatenate([middle, pack([centre])], axis=1), NAMES, crossing())
    middle_own = crossed[:, :384].astype(F32)
    got = send_all(jnp.concatenate([crossed, cot_own], axis=1), DP)
    cot_all = got[:, 512:]
    centred = got[:, :384].astype(F32) - unpack(got[:, 384:512].astype(F32), 0)
    ones = jnp.ones((1, 384), F32)
    cols = pack([row_dot(centred * centred, ones), row_dot(centred, ones)], 64 * core)
    centred = (centred * gain_b).astype(BF)
    message = jnp.stack(
        [
            jnp.concatenate(
                [
                    dot(centred, up_second[:, at : at + 768]).astype(BF),
                    contract_cols(cot_all, down_second[at : at + 768]).astype(BF),
                    cols,
                    jnp.tile(tile_rows(u_b[at : at + 768], 16), (16, 1)),
                ],
                axis=1,
            )
            for at in (0, 768)
        ]
    )
    got = exchange(message, "core")
    part = jnp.sum(got.astype(F32), axis=0).astype(BF)
    sums = jnp.sum(exchange(part.reshape(16, 16, 1792), ROW).astype(F32), axis=0)
    gain_up_b = sums[:6, 1664:].reshape(1, 768)
    off = unpack_pair(sums[:, 1536:1664], 1) / D
    rstd_b = lax.rsqrt(unpack_pair(sums[:, 1536:1664], 0) / D - off * off + EPS)
    hidden_b = (sums[:, :768] - off * gain_up_b) * rstd_b
    active_b = gelu_value(hidden_b).astype(BF)
    d_hid_b = (sums[:, 768:1536] * gelu_slope(hidden_b)).astype(BF)
    floats = d_hid_b.astype(F32)
    cols = pack(
        [
            jnp.sum(floats * gain_up_b, axis=1, keepdims=True),
            jnp.sum(floats * hidden_b, axis=1, keepdims=True),
            rstd_b,
            off,
        ],
        64 * core,
    )
    got = send_all(jnp.concatenate([d_hid_b, cols, active_b], axis=1), ROW)
    active = both_cores(got[:, 896:])
    got = both_cores(got[:, :896])
    part = contract_cols(got[0, :, :768], up_second[:, :768])
    part = part + contract_cols(got[1, :, :768], up_second[:, 768:])
    cols = got[0, :, 768:] + got[1, :, 768:]
    part_b = dot(active[0], down_second[:768]) + dot(active[1], down_second[768:])
    message = jnp.concatenate([part.astype(BF), cols, part_b.astype(BF)], axis=1)
    got = exchange(message.reshape(16, 16, 896), DP)
    sums = jnp.sum(got.astype(F32), axis=0)
    residual_out = (middle_own + sums[:, 512:]).astype(BF)
    sum_one = unpack_pair(sums[:, 384:512], 0)
    sum_two = unpack_pair(sums[:, 384:512], 1)
    cols = got[0, :, 384:512].astype(F32)
    rstd_own = unpack(cols, 2)
    mean_own = unpack(crossed[:, 384:].astype(F32), 0) + unpack(cols, 3)
    nhat_b = (middle_own - mean_own) * rstd_own
    grad_own = cot_own.astype(F32) + rstd_own * (
        sums[:, :384] * gain_b - sum_one / D - nhat_b * (sum_two / D)
    )

    crossed = lax.ppermute(
        grad_own.astype(BF), NAMES, [(target, source) for source, target in crossing()]
    )
    grad_all = both_cores(send_all(crossed, ROW))
    grad_cols = jnp.concatenate([grad_all[0], grad_all[1]], axis=1)
    part = contract_cols(grad_cols, down_first)
    sums = jnp.sum(exchange(part.astype(BF).reshape(16, 16, 768), DP).astype(F32), axis=0)
    d_hid_a = (sums * gelu_slope(hidden_a)).astype(BF)
    floats = d_hid_a.astype(F32)
    cols = pack(
        [
            jnp.sum(floats * gain_up_a, axis=1, keepdims=True),
            jnp.sum(floats * hidden_a, axis=1, keepdims=True),
        ],
        64 * core,
    )
    got = send_all(jnp.concatenate([d_hid_a, cols], axis=1), DP)
    part = contract_cols(got[:, :768], up_first).astype(BF)
    message = jnp.concatenate([part, got[:, 768:]], axis=1).reshape(2, 2, 64, 896)
    part = pair_sum(core, message[:, 0].reshape(128, 896), message[:, 1].reshape(128, 896))
    sums = jnp.sum(exchange(part.reshape(16, 8, 896), ROW).astype(F32), axis=0)
    sum_one = unpack_pair(sums[:, 768:], 0)
    sum_two = unpack_pair(sums[:, 768:], 1)
    stats = lax.dynamic_slice_in_dim(stats_a, own_row, 8, 0).astype(F32)
    rstd = unpack(stats, 1)
    nhat_a = (x_own.astype(F32) - unpack(stats, 0)) * rstd
    upstream = lax.dynamic_slice_in_dim(grad_cols, own_row, 8, 0).astype(F32)
    result = upstream + rstd * (sums[:, :768] * gain_a - sum_one / D - nhat_a * (sum_two / D))
    return residual_out[None], result.astype(BF)[None]


def solution(mesh):
    fine = Mesh(mesh.devices.reshape(SIZES), NAMES)
    row = ("xh", "core", "z")
    return jax.shard_map(
        per_device,
        mesh=fine,
        in_specs=(
            P(None, row, DP),
            P(DP, row),
            P(row, DP),
            P(DP),
            P(row, DP),
            P(DP, row),
            P(row),
            P(None, DP, row),
        ),
        out_specs=(P(None, DP, row), P(None, row, DP)),
        check_vma=False,
    )
```

```python
import jax
import jax.numpy as jnp
from jax import lax
from jax.sharding import Mesh, PartitionSpec as P

D = 12288
EPS = 1e-05
GELU_C0 = 0.7978845608028654
GELU_C1 = 0.044715
BF = jnp.bfloat16
F32 = jnp.float32
NAMES = ("xh", "core", "z", "y", "xl")
SIZES = (2, 2, 8, 8, 2)
ROW = ("xh", "z")
DP = ("y", "xl")
LANES = 128


def gelu_value(hidden):
    inner = jnp.tanh(GELU_C0 * (hidden + GELU_C1 * hidden * hidden * hidden))
    return 0.5 * hidden * (1.0 + inner)


def gelu_slope(hidden):
    inner = jnp.tanh(GELU_C0 * (hidden + GELU_C1 * hidden * hidden * hidden))
    return 0.5 * (1.0 + inner) + 0.5 * hidden * (1.0 - inner * inner) * GELU_C0 * (
        1.0 + 3.0 * GELU_C1 * hidden * hidden
    )


def dot(left, right):
    return jnp.dot(left, right, preferred_element_type=F32)


def contract_cols(left, right):
    return lax.dot_general(left, right, (((1,), (1,)), ((), ())), preferred_element_type=F32)


def row_dot(values, row):
    return lax.dot_general(
        values,
        jnp.broadcast_to(row, (LANES, values.shape[1])),
        (((1,), (1,)), ((), ())),
        precision=lax.Precision.HIGHEST,
        preferred_element_type=F32,
    )


def split3(value):
    high = lax.reduce_precision(value, 8, 7)
    rest = value - high
    mid = lax.reduce_precision(rest, 8, 7)
    return high, mid, rest - mid


def pack(columns, first=0):
    rows = columns[0].shape[0]
    lane = lax.broadcasted_iota(jnp.int32, (rows, LANES), 1) - first
    block = jnp.zeros((rows, LANES), F32)
    for number, column in enumerate(columns):
        for part, piece in enumerate(split3(column)):
            block = jnp.where(lane == 3 * number + part, piece, block)
    return block.astype(BF)


def unpack(floats, number):
    at = 3 * number
    return floats[..., at : at + 1] + floats[..., at + 1 : at + 2] + floats[..., at + 2 : at + 3]


def unpack_pair(floats, number):
    return unpack(floats, number) + unpack(floats[..., 64:], number)


def exchange(blocks, axis):
    return lax.all_to_all(blocks, axis, 0, 0)


def send_all(rows, axis):
    got = exchange(jnp.broadcast_to(rows[None], (16,) + rows.shape), axis)
    return got.reshape(16 * rows.shape[0], rows.shape[1])


def both_cores(values):
    return lax.all_gather(values, "core", axis=0, tiled=False)


def pair_sum(core, first, second):
    both = both_cores(jnp.where(core == 0, second, first))
    kept = jnp.where(core == 0, first, second)
    return (kept.astype(F32) + jnp.where(core == 0, both[1], both[0]).astype(F32)).astype(BF)


def tile_rows(vector, rows):
    block = vector.reshape(-1, LANES)
    return jnp.concatenate([block, jnp.zeros((rows - block.shape[0], LANES), vector.dtype)], axis=0)


def crossing():
    pairs = []
    for xh in range(2):
        for core in range(2):
            for z in range(8):
                for group in range(16):
                    source = ((xh * 2 + core) * 8 + z) * 16 + group
                    pairs.append((source, (2 * group + core) * 16 + xh * 8 + z))
    return pairs


def per_device(
    residual_in, up_first, down_first, gain_first, up_second, down_second, gain_second, cotangent
):
    core = lax.axis_index("core")
    chunk = lax.axis_index("xh") * 8 + lax.axis_index("z")
    own_row = (lax.axis_index("xh") * 16 + core * 8 + lax.axis_index("z")) * 8
    gain_a = gain_first.astype(F32)
    gain_b = gain_second.astype(F32)
    x_own = residual_in[0]
    cot_own = cotangent[0]

    u_a = dot(jnp.broadcast_to(gain_first[None], (8, 768)), up_first)[0].astype(BF)
    u_b = dot(jnp.broadcast_to(gain_second[None], (8, 384)), up_second)[0].astype(BF)
    down_sum = contract_cols(jnp.ones((8, 768), BF), down_first)[0].astype(BF)
    sums_a = jnp.concatenate([u_a.reshape(8, 96), down_sum.reshape(8, 96)], axis=0)
    sums_a = jnp.pad(sums_a, ((0, 0), (0, 32)))

    got = both_cores(send_all(x_own, ROW))
    x_all = jnp.transpose(got.reshape(2, 2, 64, 768), (1, 0, 2, 3)).reshape(256, 768)

    floats = x_all.astype(F32)
    centre = jnp.sum(floats, axis=1, keepdims=True) / 768
    centred = floats - centre
    x_cols = pack([centre, jnp.sum(centred * centred, axis=1, keepdims=True)], 96)
    lane = lax.broadcasted_iota(jnp.int32, (16, 16, LANES), 2)
    x_cols = jnp.where(lane < 96, sums_a, x_cols.reshape(16, 16, LANES))
    part = dot((centred * gain_a).astype(BF), up_first).astype(BF)
    got = exchange(jnp.concatenate([part.reshape(16, 16, 768), x_cols], axis=2), DP)
    cols = got[:, :, 864:].astype(F32)
    centres = unpack(cols, 0)
    mean_a = jnp.mean(centres, axis=0)
    off = centres - mean_a
    var_a = (jnp.sum(unpack(cols, 1), axis=0) + 768 * jnp.sum(off * off, axis=0)) / D
    rstd_a = lax.rsqrt(var_a + EPS)
    u_all = got[:, :8, 768:864].reshape(16, 1, 768).astype(F32)
    gain_up_a = jnp.sum(u_all, axis=0)
    down_sum = jnp.sum(got[:, 8:, 768:864].astype(F32), axis=0).reshape(1, 768)
    hidden_a = rstd_a * jnp.sum(got[:, :, :768].astype(F32) + off * u_all, axis=0)
    active = gelu_value(hidden_a).astype(BF)
    got = send_all(jnp.concatenate([active, pack([mean_a, rstd_a])], axis=1), DP)
    stats_a = got[:, 768:]
    active = got[:, :768]
    part = dot(active, down_first).astype(BF)
    shift = row_dot(active.astype(F32), down_sum) + unpack(stats_a.astype(F32), 0) * (D / 32)
    cols = pack([shift], 64 * core)
    part = pair_sum(
        core,
        jnp.concatenate([part[:, :384], cols], axis=1),
        jnp.concatenate([part[:, 384:], cols], axis=1),
    )
    sums = jnp.sum(exchange(part.reshape(16, 16, 512), ROW).astype(F32), axis=0)
    centre = unpack_pair(sums[:, 384:], 0) / D
    rows = lax.dynamic_slice_in_dim(x_all, chunk * 16, 16, 0)
    rows = jnp.where(core == 0, rows[:, :384], rows[:, 384:]).astype(F32)
    middle = (rows + sums[:, :384]).astype(BF)

    crossed = lax.ppermute(jnp.concatenate([middle, pack([centre])], axis=1), NAMES, crossing())
    got = send_all(jnp.concatenate([crossed, cot_own], axis=1), DP)
    cot_all = got[:, 512:]
    centred = got[:, :384].astype(F32) - unpack(got[:, 384:512].astype(F32), 0)
    ones = jnp.ones((1, 384), F32)
    cols = pack([row_dot(centred * centred, ones), row_dot(centred, ones)], 64 * core)
    centred = (centred * gain_b).astype(BF)
    message = jnp.stack(
        [
            jnp.concatenate(
                [
                    dot(centred, up_second[:, at : at + 768]).astype(BF),
                    contract_cols(cot_all, down_second[at : at + 768]).astype(BF),
                    cols,
                    jnp.tile(tile_rows(u_b[at : at + 768], 16), (16, 1)),
                ],
                axis=1,
            )
            for at in (0, 768)
        ]
    )
    got = exchange(message, "core")
    part = jnp.sum(got.astype(F32), axis=0).astype(BF)
    sums = jnp.sum(exchange(part.reshape(16, 16, 1792), ROW).astype(F32), axis=0)
    gain_up_b = sums[:6, 1664:].reshape(1, 768)
    off = unpack_pair(sums[:, 1536:1664], 1) / D
    rstd_b = lax.rsqrt(unpack_pair(sums[:, 1536:1664], 0) / D - off * off + EPS)
    hidden_b = (sums[:, :768] - off * gain_up_b) * rstd_b
    active_b = gelu_value(hidden_b).astype(BF)
    d_hid_b = (sums[:, 768:1536] * gelu_slope(hidden_b)).astype(BF)
    floats = d_hid_b.astype(F32)
    cols = pack(
        [
            jnp.sum(floats * gain_up_b, axis=1, keepdims=True),
            jnp.sum(floats * hidden_b, axis=1, keepdims=True),
            rstd_b,
            off,
        ],
        64 * core,
    )
    got = send_all(jnp.concatenate([d_hid_b, cols, active_b], axis=1), ROW)
    active = both_cores(got[:, 896:])
    got = both_cores(got[:, :896])
    part = contract_cols(got[0, :, :768], up_second[:, :768])
    part = part + contract_cols(got[1, :, :768], up_second[:, 768:])
    cols = got[0, :, 768:] + got[1, :, 768:]
    part_b = dot(active[0], down_second[:768]) + dot(active[1], down_second[768:])
    message = jnp.concatenate([part.astype(BF), cols, part_b.astype(BF)], axis=1)
    got = exchange(message.reshape(16, 16, 896), DP)
    got, crossed, cot_own = lax.optimization_barrier((got, crossed, cot_own))
    middle_own = crossed[:, :384].astype(F32)
    sums = jnp.sum(got.astype(F32), axis=0)
    residual_out = (middle_own + sums[:, 512:]).astype(BF)
    sum_one = unpack_pair(sums[:, 384:512], 0)
    sum_two = unpack_pair(sums[:, 384:512], 1)
    cols = got[0, :, 384:512].astype(F32)
    rstd_own = unpack(cols, 2)
    mean_own = unpack(crossed[:, 384:].astype(F32), 0) + unpack(cols, 3)
    nhat_b = (middle_own - mean_own) * rstd_own
    grad_own = cot_own.astype(F32) + rstd_own * (
        sums[:, :384] * gain_b - sum_one / D - nhat_b * (sum_two / D)
    )

    crossed = lax.ppermute(
        grad_own.astype(BF), NAMES, [(target, source) for source, target in crossing()]
    )
    grad_all = both_cores(send_all(crossed, ROW))
    grad_cols = jnp.concatenate([grad_all[0], grad_all[1]], axis=1)
    part = contract_cols(grad_cols, down_first)
    sums = jnp.sum(exchange(part.astype(BF).reshape(16, 16, 768), DP).astype(F32), axis=0)
    d_hid_a = (sums * gelu_slope(hidden_a)).astype(BF)
    floats = d_hid_a.astype(F32)
    cols = pack(
        [
            jnp.sum(floats * gain_up_a, axis=1, keepdims=True),
            jnp.sum(floats * hidden_a, axis=1, keepdims=True),
        ],
        64 * core,
    )
    got = send_all(jnp.concatenate([d_hid_a, cols], axis=1), DP)
    part = contract_cols(got[:, :768], up_first).astype(BF)
    message = jnp.concatenate([part, got[:, 768:]], axis=1).reshape(2, 2, 64, 896)
    part = pair_sum(core, message[:, 0].reshape(128, 896), message[:, 1].reshape(128, 896))
    sums = jnp.sum(exchange(part.reshape(16, 8, 896), ROW).astype(F32), axis=0)
    sum_one = unpack_pair(sums[:, 768:], 0)
    sum_two = unpack_pair(sums[:, 768:], 1)
    stats = lax.dynamic_slice_in_dim(stats_a, own_row, 8, 0).astype(F32)
    rstd = unpack(stats, 1)
    nhat_a = (x_own.astype(F32) - unpack(stats, 0)) * rstd
    upstream = lax.dynamic_slice_in_dim(grad_cols, own_row, 8, 0).astype(F32)
    result = upstream + rstd * (sums[:, :768] * gain_a - sum_one / D - nhat_a * (sum_two / D))
    return residual_out[None], result.astype(BF)[None]


def solution(mesh):
    fine = Mesh(mesh.devices.reshape(SIZES), NAMES)
    row = ("xh", "core", "z")
    return jax.shard_map(
        per_device,
        mesh=fine,
        in_specs=(
            P(None, row, DP),
            P(DP, row),
            P(row, DP),
            P(DP),
            P(row, DP),
            P(DP, row),
            P(row),
            P(None, DP, row),
        ),
        out_specs=(P(None, DP, row), P(None, row, DP)),
        check_vma=False,
    )
```

```python
import jax
import jax.numpy as jnp
from jax import lax
from jax.sharding import Mesh, PartitionSpec as P

D = 12288
EPS = 1e-05
GELU_C0 = 0.7978845608028654
GELU_C1 = 0.044715
BF = jnp.bfloat16
F32 = jnp.float32
NAMES = ("xh", "core", "z", "y", "xl")
SIZES = (2, 2, 8, 8, 2)
ROW = ("xh", "z")
DP = ("y", "xl")
LANES = 128


def gelu_value(hidden):
    inner = jnp.tanh(GELU_C0 * (hidden + GELU_C1 * hidden * hidden * hidden))
    return 0.5 * hidden * (1.0 + inner)


def gelu_slope(hidden):
    inner = jnp.tanh(GELU_C0 * (hidden + GELU_C1 * hidden * hidden * hidden))
    return 0.5 * (1.0 + inner) + 0.5 * hidden * (1.0 - inner * inner) * GELU_C0 * (
        1.0 + 3.0 * GELU_C1 * hidden * hidden
    )


def dot(left, right):
    return jnp.dot(left, right, preferred_element_type=F32)


def contract_cols(left, right):
    return lax.dot_general(left, right, (((1,), (1,)), ((), ())), preferred_element_type=F32)


def row_dot(values, row):
    return lax.dot_general(
        values,
        jnp.broadcast_to(row, (LANES, values.shape[1])),
        (((1,), (1,)), ((), ())),
        precision=lax.Precision.HIGHEST,
        preferred_element_type=F32,
    )


def split3(value):
    high = lax.reduce_precision(value, 8, 7)
    rest = value - high
    mid = lax.reduce_precision(rest, 8, 7)
    return high, mid, rest - mid


def pack(columns, first=0):
    rows = columns[0].shape[0]
    lane = lax.broadcasted_iota(jnp.int32, (rows, LANES), 1) - first
    block = jnp.zeros((rows, LANES), F32)
    for number, column in enumerate(columns):
        for part, piece in enumerate(split3(column)):
            block = jnp.where(lane == 3 * number + part, piece, block)
    return block.astype(BF)


def unpack(floats, number):
    at = 3 * number
    return floats[..., at : at + 1] + floats[..., at + 1 : at + 2] + floats[..., at + 2 : at + 3]


def unpack_pair(floats, number):
    return unpack(floats, number) + unpack(floats[..., 64:], number)


def exchange(blocks, axis):
    return lax.all_to_all(blocks, axis, 0, 0)


def send_all(rows, axis):
    got = exchange(jnp.broadcast_to(rows[None], (16,) + rows.shape), axis)
    return got.reshape(16 * rows.shape[0], rows.shape[1])


def both_cores(values):
    return lax.all_gather(values, "core", axis=0, tiled=False)


def pair_sum(core, first, second):
    both = both_cores(jnp.where(core == 0, second, first))
    kept = jnp.where(core == 0, first, second)
    return (kept.astype(F32) + jnp.where(core == 0, both[1], both[0]).astype(F32)).astype(BF)


def tile_rows(vector, rows):
    block = vector.reshape(-1, LANES)
    return jnp.concatenate([block, jnp.zeros((rows - block.shape[0], LANES), vector.dtype)], axis=0)


def crossing():
    pairs = []
    for xh in range(2):
        for core in range(2):
            for z in range(8):
                for group in range(16):
                    source = ((xh * 2 + core) * 8 + z) * 16 + group
                    pairs.append((source, (2 * group + core) * 16 + xh * 8 + z))
    return pairs


def per_device(
    residual_in, up_first, down_first, gain_first, up_second, down_second, gain_second, cotangent
):
    core = lax.axis_index("core")
    chunk = lax.axis_index("xh") * 8 + lax.axis_index("z")
    own_row = (lax.axis_index("xh") * 16 + core * 8 + lax.axis_index("z")) * 8
    gain_a = gain_first.astype(F32)
    gain_b = gain_second.astype(F32)
    x_own = residual_in[0]
    cot_own = cotangent[0]

    u_a = dot(jnp.broadcast_to(gain_first[None], (8, 768)), up_first)[0].astype(BF)
    u_b = dot(jnp.broadcast_to(gain_second[None], (8, 384)), up_second)[0].astype(BF)
    down_sum = contract_cols(jnp.ones((8, 768), BF), down_first)[0].astype(BF)
    sums_a = jnp.concatenate([u_a.reshape(8, 96), down_sum.reshape(8, 96)], axis=0)
    sums_a = jnp.pad(sums_a, ((0, 0), (0, 32)))

    got = both_cores(send_all(x_own, ROW))
    x_all = jnp.transpose(got.reshape(2, 2, 64, 768), (1, 0, 2, 3)).reshape(256, 768)

    floats = x_all.astype(F32)
    centre = jnp.sum(floats, axis=1, keepdims=True) / 768
    centred = floats - centre
    x_cols = pack([centre, jnp.sum(centred * centred, axis=1, keepdims=True)], 96)
    lane = lax.broadcasted_iota(jnp.int32, (16, 16, LANES), 2)
    x_cols = jnp.where(lane < 96, sums_a, x_cols.reshape(16, 16, LANES))
    part = dot((centred * gain_a).astype(BF), up_first).astype(BF)
    got = exchange(jnp.concatenate([part.reshape(16, 16, 768), x_cols], axis=2), DP)
    cols = got[:, :, 864:].astype(F32)
    centres = unpack(cols, 0)
    mean_a = jnp.mean(centres, axis=0)
    off = centres - mean_a
    var_a = (jnp.sum(unpack(cols, 1), axis=0) + 768 * jnp.sum(off * off, axis=0)) / D
    rstd_a = lax.rsqrt(var_a + EPS)
    u_all = got[:, :8, 768:864].reshape(16, 1, 768).astype(F32)
    gain_up_a = jnp.sum(u_all, axis=0)
    down_sum = jnp.sum(got[:, 8:, 768:864].astype(F32), axis=0).reshape(1, 768)
    hidden_a = rstd_a * jnp.sum(got[:, :, :768].astype(F32) + off * u_all, axis=0)
    active = gelu_value(hidden_a).astype(BF)
    got = send_all(jnp.concatenate([active, pack([mean_a, rstd_a])], axis=1), DP)
    stats_a = got[:, 768:]
    active = got[:, :768]
    part = dot(active, down_first).astype(BF)
    shift = row_dot(active.astype(F32), down_sum) + unpack(stats_a.astype(F32), 0) * (D / 32)
    cols = pack([shift], 64 * core)
    part = pair_sum(
        core,
        jnp.concatenate([part[:, :384], cols], axis=1),
        jnp.concatenate([part[:, 384:], cols], axis=1),
    )
    sums = jnp.sum(exchange(part.reshape(16, 16, 512), ROW).astype(F32), axis=0)
    centre = unpack_pair(sums[:, 384:], 0) / D
    rows = lax.dynamic_slice_in_dim(x_all, chunk * 16, 16, 0)
    rows = jnp.where(core == 0, rows[:, :384], rows[:, 384:]).astype(F32)
    middle = (rows + sums[:, :384]).astype(BF)

    crossed = lax.ppermute(jnp.concatenate([middle, pack([centre])], axis=1), NAMES, crossing())
    got = send_all(jnp.concatenate([crossed, cot_own], axis=1), DP)
    cot_all = got[:, 512:]
    centred = got[:, :384].astype(F32) - unpack(got[:, 384:512].astype(F32), 0)
    ones = jnp.ones((1, 384), F32)
    cols = pack([row_dot(centred * centred, ones), row_dot(centred, ones)], 64 * core)
    centred = (centred * gain_b).astype(BF)
    halves = [
        (
            jnp.concatenate([dot(centred, up_second[:, at : at + 768]).astype(BF), cols], axis=1),
            jnp.concatenate(
                [
                    contract_cols(cot_all, down_second[at : at + 768]).astype(BF),
                    jnp.tile(tile_rows(u_b[at : at + 768], 16), (16, 1)),
                ],
                axis=1,
            ),
        )
        for at in (0, 768)
    ]
    part, part_d = (pair_sum(core, first, second) for first, second in zip(*halves))
    part = jnp.concatenate(
        [part[:, :768], part_d[:, :768], part[:, 768:], part_d[:, 768:]], axis=1
    )
    sums = jnp.sum(exchange(part.reshape(16, 16, 1792), ROW).astype(F32), axis=0)
    gain_up_b = sums[:6, 1664:].reshape(1, 768)
    off = unpack_pair(sums[:, 1536:1664], 1) / D
    rstd_b = lax.rsqrt(unpack_pair(sums[:, 1536:1664], 0) / D - off * off + EPS)
    hidden_b = (sums[:, :768] - off * gain_up_b) * rstd_b
    active_b = gelu_value(hidden_b).astype(BF)
    d_hid_b = (sums[:, 768:1536] * gelu_slope(hidden_b)).astype(BF)
    floats = d_hid_b.astype(F32)
    cols = pack(
        [
            jnp.sum(floats * gain_up_b, axis=1, keepdims=True),
            jnp.sum(floats * hidden_b, axis=1, keepdims=True),
            rstd_b,
            off,
        ],
        64 * core,
    )
    got = send_all(jnp.concatenate([d_hid_b, cols, active_b], axis=1), ROW)
    active = both_cores(got[:, 896:])
    got = both_cores(got[:, :896])
    part = contract_cols(got[0, :, :768], up_second[:, :768])
    part = part + contract_cols(got[1, :, :768], up_second[:, 768:])
    cols = got[0, :, 768:] + got[1, :, 768:]
    part_b = dot(active[0], down_second[:768]) + dot(active[1], down_second[768:])
    message = jnp.concatenate([part.astype(BF), cols, part_b.astype(BF)], axis=1)
    got = exchange(message.reshape(16, 16, 896), DP)
    got, crossed, cot_own = lax.optimization_barrier((got, crossed, cot_own))
    middle_own = crossed[:, :384].astype(F32)
    sums = jnp.sum(got.astype(F32), axis=0)
    residual_out = (middle_own + sums[:, 512:]).astype(BF)
    sum_one = unpack_pair(sums[:, 384:512], 0)
    sum_two = unpack_pair(sums[:, 384:512], 1)
    cols = got[0, :, 384:512].astype(F32)
    rstd_own = unpack(cols, 2)
    mean_own = unpack(crossed[:, 384:].astype(F32), 0) + unpack(cols, 3)
    nhat_b = (middle_own - mean_own) * rstd_own
    grad_own = cot_own.astype(F32) + rstd_own * (
        sums[:, :384] * gain_b - sum_one / D - nhat_b * (sum_two / D)
    )

    crossed = lax.ppermute(
        grad_own.astype(BF), NAMES, [(target, source) for source, target in crossing()]
    )
    grad_all = both_cores(send_all(crossed, ROW))
    grad_cols = jnp.concatenate([grad_all[0], grad_all[1]], axis=1)
    part = contract_cols(grad_cols, down_first)
    sums = jnp.sum(exchange(part.astype(BF).reshape(16, 16, 768), DP).astype(F32), axis=0)
    d_hid_a = (sums * gelu_slope(hidden_a)).astype(BF)
    floats = d_hid_a.astype(F32)
    cols = pack(
        [
            jnp.sum(floats * gain_up_a, axis=1, keepdims=True),
            jnp.sum(floats * hidden_a, axis=1, keepdims=True),
        ],
        64 * core,
    )
    got = send_all(jnp.concatenate([d_hid_a, cols], axis=1), DP)
    part = contract_cols(got[:, :768], up_first).astype(BF)
    message = jnp.concatenate([part, got[:, 768:]], axis=1).reshape(2, 2, 64, 896)
    part = pair_sum(core, message[:, 0].reshape(128, 896), message[:, 1].reshape(128, 896))
    sums = jnp.sum(exchange(part.reshape(16, 8, 896), ROW).astype(F32), axis=0)
    sum_one = unpack_pair(sums[:, 768:], 0)
    sum_two = unpack_pair(sums[:, 768:], 1)
    stats = lax.dynamic_slice_in_dim(stats_a, own_row, 8, 0).astype(F32)
    rstd = unpack(stats, 1)
    nhat_a = (x_own.astype(F32) - unpack(stats, 0)) * rstd
    upstream = lax.dynamic_slice_in_dim(grad_cols, own_row, 8, 0).astype(F32)
    result = upstream + rstd * (sums[:, :768] * gain_a - sum_one / D - nhat_a * (sum_two / D))
    return residual_out[None], result.astype(BF)[None]


def solution(mesh):
    fine = Mesh(mesh.devices.reshape(SIZES), NAMES)
    row = ("xh", "core", "z")
    return jax.shard_map(
        per_device,
        mesh=fine,
        in_specs=(
            P(None, row, DP),
            P(DP, row),
            P(row, DP),
            P(DP),
            P(row, DP),
            P(DP, row),
            P(row),
            P(None, DP, row),
        ),
        out_specs=(P(None, DP, row), P(None, row, DP)),
        check_vma=False,
    )
```
